32 devices in a mesh: gy: 2 (over x), gx: 4 (over z), gz: 4 (over y, core).
Axes of the slice: x: 2, y: 2, z: 4, core: 2. Of those that a mesh axis runs over, the one named last changes fastest.
Arguments:
- adjoint: float32 [3, 64, 256, 512], P(None, 'gx', 'gy', 'gz'), may hold values from -6 to 6
- base_flow: float32 [3, 64, 256, 512], P(None, 'gx', 'gy', 'gz'), may hold values from -4 to 4
- viscosity: float32 [64, 256, 512], P('gx', 'gy', 'gz'), may hold values from 0.3 to 3
- first_matrix: float32 [256, 256], replicated, may hold values from -0.375 to 0.375
- second_matrix: float32 [256, 256], replicated, may hold values from -0.375 to 0.375
Outputs:
- earlier: float32 [3, 64, 256, 512], P(None, 'gx', 'gy', 'gz')
The draws below stay inside these ranges and needn't reach their ends.
All inputs are finite; a program needn't handle non-finite values.
Results may differ from the reference program's by a relative error of at most 0.00012.
Values sent between devices are 32-bit elements; how exact they have to be, the bound alone decides.
A program may use at most 128 MiB of HBM per device.

```python
import math
import jax
import jax.numpy as jnp
from jax import lax

NY = 256
STEPS = 2
NX = 64
NZ = 512


def steps_of(rng, shape, shards, low, top_value):
    def one(axis_at, blocks):
        heights = jax.random.uniform(jax.random.fold_in(jax.random.fold_in(rng, 6), axis_at), (blocks,), jnp.float32, low / len(shards), top_value / len(shards))
        return jnp.repeat(jnp.exp(heights), shape[axis_at] // blocks).reshape((-1,) + (1,) * (len(shape) - axis_at - 1))

    factor_of = one(*shards[0])
    for cut in shards[1:]:
        factor_of = factor_of * one(*cut)
    return factor_of


def gaussian(stream_key, extent, spread, limit, cuts=(), kind=jnp.bfloat16):
    values = jax.random.normal(stream_key, extent, jnp.float32) * spread
    if len(cuts) > 0:
        values = steps_of(stream_key, extent, cuts, -0.22, 0.18) * values
    return jnp.clip(values, min=-limit, max=limit).astype(kind)


def setup_inputs(seed: int = 0) -> dict:
    arg_keys = jax.random.split(jax.random.key(seed), 6)
    adjoint = gaussian(arg_keys[0], (3, NX, NY, NZ), 1.0, 6.0, ((1, 4), (2, 2), (3, 4)), jnp.float32)
    base_flow = gaussian(arg_keys[1], (3, NX, NY, NZ), 1.0, 4.0, ((1, 4), (2, 2), (3, 4)), jnp.float32)
    viscosity = jnp.clip(jnp.exp(math.log(3.0) - 2.3025851 * jax.random.uniform(arg_keys[2], (NX, NY, NZ), jnp.float32) ** steps_of(arg_keys[2], (NX, NY, NZ), ((0, 4), (1, 2), (2, 4)), -0.2, 0.2)), 0.3, 3.0)
    first_matrix = gaussian(arg_keys[3], (NY, NY), NY ** -0.5, 0.375, (), jnp.float32)
    second_matrix = gaussian(arg_keys[4], (NY, NY), NY ** -0.5, 0.375, (), jnp.float32)
    return {"adjoint": adjoint, "base_flow": base_flow, "viscosity": viscosity, "first_matrix": first_matrix, "second_matrix": second_matrix}


advect_scale = 0.25
diffuse_scale = 0.1


def offset_view(values, along_x, along_z):
    return jnp.roll(values, (-along_x, -along_z), axis=(1, 3))


def advance_state(current, velocity, kinematic, visc_slope, matrices):
    derived = jnp.einsum("kij,cxjz->kcxiz", matrices, current, precision=lax.Precision.HIGHEST)
    east = offset_view(current, 1, 0)
    west = offset_view(current, -1, 0)
    stream_slope = (8.0 * (east - west) - (offset_view(current, 2, 0) - offset_view(current, -2, 0))) / 12.0
    upper = offset_view(current, 0, 1)
    lower = offset_view(current, 0, -1)
    span_slope = (8.0 * (upper - lower) - (offset_view(current, 0, 2) - offset_view(current, 0, -2))) / 12.0
    stream_flux = 0.5 * (kinematic + offset_view(kinematic, 1, 0)) * (east - current) - 0.5 * (offset_view(kinematic, -1, 0) + kinematic) * (current - west)
    span_flux = 0.5 * (kinematic + offset_view(kinematic, 0, 1)) * (upper - current) - 0.5 * (offset_view(kinematic, 0, -1) + kinematic) * (current - lower)
    updated = current + advect_scale * (velocity[0:1] * stream_slope + velocity[1:2] * derived[0] + velocity[2:3] * span_slope) + diffuse_scale * (stream_flux + span_flux + kinematic * derived[1] + visc_slope * derived[0])
    rows_all = jnp.arange(NY)
    inside = ((rows_all > 0) & (rows_all < NY - 1)).astype(current.dtype).reshape(1, 1, NY, 1)
    return updated * inside


def reference(adjoint, base_flow, viscosity, first_matrix, second_matrix):
    matrices = jnp.stack([first_matrix, second_matrix])
    kinematic = viscosity[None]
    visc_slope = jnp.einsum("ij,cxjz->cxiz", first_matrix, kinematic, precision=lax.Precision.HIGHEST)
    current = adjoint
    for step_index in range(STEPS):
        current = advance_state(current, base_flow, kinematic, visc_slope, matrices)
    return current
```

```python
import jax
import jax.numpy as jnp
from jax import lax
from jax.experimental import pallas as pl
from jax.experimental.pallas import tpu as pltpu
from jax.sharding import PartitionSpec as P

STEPS = 2
MESH = pl.DeviceIdType.MESH
F32 = jnp.float32
BF16 = jnp.bfloat16


def kernel(
    adj, flow, visc, first_m, second_m, out,
    send, state, mid, coef, late, back, matrix, rhs, derived,
    edge_out, edges, outer, rim_lo, rim_hi, edges1, inner1, outer1,
    swap_s, swap_r, edge_s, edge_r, rim_s, rim_r, ret_s, ret_r,
):
    _, cells, half_rows, lanes = adj.shape
    rows = 2 * half_rows
    half = lanes // 2
    pairs = cells // 2
    chunk = 32
    ngx, ngz = lax.axis_size("gx"), lax.axis_size("gz")
    gy, gx, gz = lax.axis_index("gy"), lax.axis_index("gx"), lax.axis_index("gz")
    upper = lax.rem(gy + gz, 2)
    peer = (1 - gy, gx, gz)
    left = (gy, lax.rem(gx + ngx - 1, ngx), gz)
    right = (gy, lax.rem(gx + 1, ngx), gz)
    beside = (gy, gx, lax.rem(gz + ngz - 1 + 2 * upper, ngz))
    mine = pl.ds(pl.multiple_of(gy * half_rows, half_rows), half_rows)
    other = pl.ds(pl.multiple_of((1 - gy) * half_rows, half_rows), half_rows)

    def remote(src, dst, s, r, device):
        return pltpu.make_async_remote_copy(
            src_ref=src, dst_ref=dst, send_sem=s, recv_sem=r, device_id=device, device_id_type=MESH
        )

    def swap(p):
        return remote(send.at[p], state.at[p + 1, :, mine, :], swap_s.at[p], swap_r.at[p], peer)

    def give_back(p):
        return remote(late.at[p, :, other, :], back.at[p], ret_s.at[p], ret_r.at[p], peer)

    swap_edges = remote(edge_out, edges.at[:, mine, :], edge_s.at[0], edge_r.at[0], peer)
    pass_edge = remote(edges.at[1], outer, edge_s.at[1], edge_r.at[1], beside)
    swap_inner1 = remote(edges1.at[0], inner1, edge_s.at[2], edge_r.at[2], peer)
    pass_outer1 = remote(edges1.at[1], outer1, edge_s.at[3], edge_r.at[3], beside)
    rim_left0 = remote(
        state.at[1, 0:4], state.at[pairs + 1, 0:4], rim_s.at[0], rim_r.at[0], left
    )
    rim_right0 = remote(state.at[pairs, 0:4], state.at[0, 0:4], rim_s.at[1], rim_r.at[1], right)
    rim_left1 = remote(mid.at[1], mid.at[pairs + 1], rim_s.at[2], rim_r.at[2], left)
    rim_right1 = remote(mid.at[pairs], mid.at[0], rim_s.at[3], rim_r.at[3], right)

    barrier = pltpu.get_barrier_semaphore()
    for device in (peer, left, right, beside):
        pl.semaphore_signal(barrier, inc=1, device_id=device, device_id_type=MESH)
    pl.semaphore_wait(barrier, 4)

    lane = lax.broadcasted_iota(jnp.int32, (half_rows, lanes), 1)
    is_upper = jnp.full((half_rows, lanes), upper, jnp.int32) == 1
    in_slot = lax.rem(lane, half) // 2
    far = half + 2

    def turn(values, shift):
        return pltpu.roll(values, lax.rem(shift + 2 * lanes, lanes), 1)

    def pack(p):
        for f in range(7):
            if f < 3:
                even, odd = adj[f, 2 * p], adj[f, 2 * p + 1]
            elif f == 3:
                even, odd = visc[2 * p], visc[2 * p + 1]
            else:
                even, odd = flow[f - 4, 2 * p], flow[f - 4, 2 * p + 1]
            lows = jnp.where(lane < half, even, pltpu.roll(odd, half, 1))
            highs = jnp.where(lane < half, pltpu.roll(even, half, 1), odd)
            keep = jnp.where(is_upper, highs, lows)
            give = jnp.where(is_upper, lows, highs)
            state[p + 1, f, mine, :] = keep
            send[p, f] = give
            if f < 4:
                k = f * pairs + p
                slot = in_slot == k
                near_shift = 2 * k + far * upper
                far_shift = 2 * k + far * (1 - upper)
                edges[0, mine, :] = jnp.where(slot, turn(give, near_shift), edges[0, mine, :])
                edges[1, mine, :] = jnp.where(slot, turn(keep, near_shift), edges[1, mine, :])
                edge_out[0] = jnp.where(slot, turn(keep, far_shift), edge_out[0])
                edge_out[1] = jnp.where(slot, turn(give, far_shift), edge_out[1])

    zeros = jnp.zeros((half_rows, lanes), F32)
    for s in range(2):
        edges[s, mine, :] = zeros
        edge_out[s] = zeros
    pack(0)
    swap(0).start()

    @pl.loop(1, pairs)
    def _(i):
        p = pairs - i
        pack(p)

        @pl.when(i <= 1)
        def _():
            swap(p).start()

    swap_edges.start()
    swap(pairs - 2).start()

    @pl.loop(1, pairs - 2)
    def _(p):
        swap(p).start()

    for s, source in enumerate((first_m, second_m)):
        values = source[...]
        high = values.astype(BF16)
        low = (values - high.astype(F32)).astype(BF16)
        block = slice(s * rows, (s + 1) * rows)
        matrix[block, 0:rows] = high
        matrix[block, rows : 2 * rows] = high
        matrix[block, 2 * rows : 3 * rows] = low
    edges1[...] = jnp.zeros(edges1.shape, F32)

    def split(source, place, count):
        for c in range(count):
            values = source[place, c]
            high = values.astype(BF16)
            low = (values - high.astype(F32)).astype(BF16)
            columns = slice(c * lanes, (c + 1) * lanes)
            rhs[0:rows, columns] = high
            rhs[rows : 2 * rows, columns] = low
            rhs[2 * rows : 3 * rows, columns] = high
        width = count * lanes
        derived[:, 0:width] = jnp.dot(
            matrix[...], rhs[:, 0:width], preferred_element_type=F32
        )

    clane = lax.broadcasted_iota(jnp.int32, (chunk, lanes), 1)
    crow = lax.broadcasted_iota(jnp.int32, (chunk, lanes), 0)
    lower_lanes = clane < half
    in_half = lax.rem(clane, half)
    cslot = lax.rem(clane, half) // 2

    def join_rims(inner, outside):
        choose = jnp.full((rows, lanes), upper, jnp.int32) == 1
        rim_lo[...] = jnp.where(choose, inner, outside)
        rim_hi[...] = jnp.where(choose, outside, inner)

    def x_views(current, before, after):
        east = pltpu.roll(jnp.where(lower_lanes, after, current), half, 1)
        west = pltpu.roll(jnp.where(lower_lanes, current, before), half, 1)
        return east, west

    def z_rims(k, at):
        return turn(rim_lo[at, :], lanes - 2 - 2 * k), turn(rim_hi[at, :], half - 2 * k)

    def z_views(current, rims, step):
        under = jnp.where(in_half >= half - step, rims[0], current)
        over = jnp.where(in_half < step, rims[1], current)
        return pltpu.roll(under, step, 1), pltpu.roll(over, lanes - step, 1)

    def coefficients(p):
        @pl.loop(0, rows // chunk)
        def _(r):
            at = pl.ds(pl.multiple_of(r * chunk, chunk), chunk)
            centre = state[p + 1, 3, at, :]
            east, west = x_views(centre, state[p, 3, at, :], state[p + 2, 3, at, :])
            lower, above = z_views(centre, z_rims(3 * pairs + p, at), 1)
            ve, vw = 0.05 * (centre + east), 0.05 * (centre + west)
            vu, vl = 0.05 * (centre + above), 0.05 * (centre + lower)
            bx, by, bz = state[p + 1, 4, at, :], state[p + 1, 5, at, :], state[p + 1, 6, at, :]
            bx6, bz6 = bx * (1.0 / 6.0), bz * (1.0 / 6.0)
            coef[p, 0, at, :] = 1.0 - (ve + vw) - (vu + vl)
            coef[p, 1, at, :] = bx6 + ve
            coef[p, 2, at, :] = vw - bx6
            coef[p, 3, at, :] = bx * (1.0 / 48.0)
            coef[p, 4, at, :] = bz6 + vu
            coef[p, 5, at, :] = vl - bz6
            coef[p, 6, at, :] = bz * (1.0 / 48.0)
            coef[p, 7, at, :] = 0.25 * by + 0.1 * derived[at, 3 * lanes : 4 * lanes]
            coef[p, 8, at, :] = 0.1 * centre

    def advance(source, p, target, place, with_edges):
        @pl.loop(0, rows // chunk)
        def _(r):
            at = pl.ds(pl.multiple_of(r * chunk, chunk), chunk)
            at2 = pl.ds(pl.multiple_of(rows + r * chunk, chunk), chunk)
            row = crow + r * chunk
            inside = (row > 0) & (row < rows - 1)
            cs = [coef[p, n, at, :] for n in range(9)]
            for c in range(3):
                k = c * pairs + p
                current = source[p + 1, c, at, :]
                before, after = source[p, c, at, :], source[p + 2, c, at, :]
                east, west = x_views(current, before, after)
                rims = z_rims(k, at)
                lower, above = z_views(current, rims, 1)
                lower2, above2 = z_views(current, rims, 2)
                columns = slice(c * lanes, (c + 1) * lanes)
                value = (
                    cs[0] * current
                    + cs[1] * east
                    + cs[2] * west
                    + cs[3] * (before - after)
                    + cs[4] * above
                    + cs[5] * lower
                    + cs[6] * (lower2 - above2)
                    + cs[7] * derived[at, columns]
                    + cs[8] * derived[at2, columns]
                )
                value = jnp.where(inside, value, 0.0)
                target[place, c, at, :] = value
                if with_edges:
                    slot = cslot == k
                    edges1[0, at, :] = jnp.where(
                        slot, turn(value, 2 * k + far * (1 - upper)), edges1[0, at, :]
                    )
                    edges1[1, at, :] = jnp.where(
                        slot, turn(value, 2 * k + far * upper), edges1[1, at, :]
                    )

    swap(0).wait_recv()
    rim_left0.start()
    swap(pairs - 1).wait_recv()
    rim_right0.start()
    swap_edges.wait_recv()
    pass_edge.start()
    pass_edge.wait_recv()
    join_rims(edges[0], outer[...])

    @pl.loop(0, pairs)
    def _(i):
        p = jnp.where(i == 0, pairs - 1, i - 1)

        @pl.when(i == 0)
        def _():
            swap(pairs - 2).wait_recv()
            rim_left0.wait_recv()

        @pl.when(i == 1)
        def _():
            swap(1).wait_recv()
            rim_right0.wait_recv()

        @pl.when((i >= 2) & (i < pairs - 2))
        def _():
            swap(i).wait_recv()

        split(state, p + 1, 4)
        coefficients(p)
        advance(state, p, mid, p + 1, True)

        @pl.when(i == 0)
        def _():
            rim_right1.start()

        @pl.when(i == 1)
        def _():
            rim_left1.start()

    swap_inner1.start()
    pass_outer1.start()
    swap_inner1.wait_recv()
    pass_outer1.wait_recv()
    rim_left1.wait_recv()
    rim_right1.wait_recv()
    join_rims(inner1[...], outer1[...])

    @pl.loop(0, pairs)
    def _(p):
        split(mid, p + 1, 3)
        advance(mid, p, late, p, False)
        give_back(p).start()

    @pl.loop(0, pairs)
    def _(p):
        give_back(p).wait_recv()
        for c in range(3):
            keep = late[p, c, mine, :]
            got = back[p, c]
            lows = jnp.where(is_upper, got, keep)
            highs = jnp.where(is_upper, keep, got)
            out[c, 2 * p] = jnp.where(lane < half, lows, pltpu.roll(highs, half, 1))
            out[c, 2 * p + 1] = jnp.where(lane < half, pltpu.roll(lows, half, 1), highs)

    @pl.loop(0, pairs)
    def _(p):
        swap(p).wait_send()
        give_back(p).wait_send()

    for copy in (
        swap_edges, pass_edge, swap_inner1, pass_outer1,
        rim_left0, rim_right0, rim_left1, rim_right1,
    ):
        copy.wait_send()


def per_device(adjoint, base_flow, viscosity, first_matrix, second_matrix):
    _, cells, half_rows, lanes = adjoint.shape
    rows, pairs = 2 * half_rows, cells // 2
    plane = (rows, lanes)
    vmem = pl.BlockSpec(memory_space=pltpu.VMEM)
    dma = pltpu.SemaphoreType.DMA
    return pl.pallas_call(
        kernel,
        out_shape=jax.ShapeDtypeStruct(adjoint.shape, F32),
        in_specs=[vmem] * 5,
        out_specs=vmem,
        scratch_shapes=[
            pltpu.VMEM((pairs, 7, half_rows, lanes), F32),
            pltpu.VMEM((pairs + 2, 7) + plane, F32),
            pltpu.VMEM((pairs + 2, 3) + plane, F32),
            pltpu.VMEM((pairs, 9) + plane, F32),
            pltpu.VMEM((pairs, 3) + plane, F32),
            pltpu.VMEM((pairs, 3, half_rows, lanes), F32),
            pltpu.VMEM((2 * rows, 3 * rows), BF16),
            pltpu.VMEM((3 * rows, 4 * lanes), BF16),
            pltpu.VMEM((2 * rows, 4 * lanes), F32),
            pltpu.VMEM((2, half_rows, lanes), F32),
            pltpu.VMEM((2,) + plane, F32),
            pltpu.VMEM(plane, F32),
            pltpu.VMEM(plane, F32),
            pltpu.VMEM(plane, F32),
            pltpu.VMEM((2,) + plane, F32),
            pltpu.VMEM(plane, F32),
            pltpu.VMEM(plane, F32),
            dma((pairs,)), dma((pairs,)),
            dma((4,)), dma((4,)),
            dma((4,)), dma((4,)),
            dma((pairs,)), dma((pairs,)),
        ],
        compiler_params=pltpu.CompilerParams(
            collective_id=0, has_side_effects=True, vmem_limit_bytes=56 * 1024 * 1024
        ),
        name="adjoint_steps",
    )(adjoint, base_flow, viscosity, first_matrix, second_matrix)


def solution(mesh):
    return jax.shard_map(
        per_device,
        mesh=mesh,
        in_specs=(
            P(None, "gx", "gy", "gz"),
            P(None, "gx", "gy", "gz"),
            P("gx", "gy", "gz"),
            P(),
            P(),
        ),
        out_specs=P(None, "gx", "gy", "gz"),
        check_vma=False,
    )
```

```python
import jax
import jax.numpy as jnp
from jax import lax
from jax.experimental import pallas as pl
from jax.experimental.pallas import tpu as pltpu
from jax.sharding import PartitionSpec as P

STEPS = 2
MESH = pl.DeviceIdType.MESH
F32 = jnp.float32
BF16 = jnp.bfloat16


def kernel(
    adj_in, flow_in, visc_in, first_m, second_m, out_hbm,
    adj, flow, visc, out,
    send, state, mid, coef, late, back, matrix, rhs, derived,
    edge_out, edges, outer, rim_lo, rim_hi, edges1, inner1, outer1, rim1_lo, rim1_hi,
    swap_s, swap_r, edge_s, edge_r, rim_s, rim_r, ret_s, ret_r, load_s, store_s,
):
    _, cells, half_rows, lanes = adj_in.shape
    rows = 2 * half_rows
    half = lanes // 2
    pairs = cells // 2
    chunk = 32
    early = pairs * 3 // 8
    ngx, ngz = lax.axis_size("gx"), lax.axis_size("gz")
    gy, gx, gz = lax.axis_index("gy"), lax.axis_index("gx"), lax.axis_index("gz")
    upper = lax.rem(gy + gz, 2)
    peer = (1 - gy, gx, gz)
    left = (gy, lax.rem(gx + ngx - 1, ngx), gz)
    right = (gy, lax.rem(gx + 1, ngx), gz)
    beside = (gy, gx, lax.rem(gz + ngz - 1 + 2 * upper, ngz))
    mine = pl.ds(pl.multiple_of(gy * half_rows, half_rows), half_rows)
    other = pl.ds(pl.multiple_of((1 - gy) * half_rows, half_rows), half_rows)

    def remote(src, dst, s, r, device):
        return pltpu.make_async_remote_copy(
            src_ref=src, dst_ref=dst, send_sem=s, recv_sem=r, device_id=device, device_id_type=MESH
        )

    def swap(p):
        return remote(send.at[p], state.at[p + 1, :, mine, :], swap_s.at[p], swap_r.at[p], peer)

    def give_back(p):
        return remote(late.at[p, :, other, :], back.at[p], ret_s.at[p], ret_r.at[p], peer)

    swap_edges = remote(edge_out, edges.at[:, mine, :], edge_s.at[0], edge_r.at[0], peer)
    pass_edge = remote(edges.at[1], outer, edge_s.at[1], edge_r.at[1], beside)

    def edge_copies(g):
        s, r = edge_s.at[2 + 2 * g], edge_r.at[2 + 2 * g]
        inner = remote(edges1.at[g, 0], inner1.at[g], s, r, peer)
        s, r = edge_s.at[3 + 2 * g], edge_r.at[3 + 2 * g]
        return inner, remote(edges1.at[g, 1], outer1.at[g], s, r, beside)

    def loads(p):
        cells_of = pl.ds(2 * p, 2)
        return (
            pltpu.make_async_copy(adj_in.at[:, cells_of], adj.at[:, cells_of], load_s.at[0, p]),
            pltpu.make_async_copy(visc_in.at[cells_of], visc.at[cells_of], load_s.at[1, p]),
            pltpu.make_async_copy(flow_in.at[:, cells_of], flow.at[:, cells_of], load_s.at[2, p]),
        )

    def store(p):
        cells_of = pl.ds(2 * p, 2)
        return pltpu.make_async_copy(out.at[:, cells_of], out_hbm.at[:, cells_of], store_s.at[p])

    for copy in loads(0):
        copy.start()

    @pl.loop(1, pairs)
    def _(i):
        for copy in loads(pairs - i):
            copy.start()

    rim_left0 = remote(
        state.at[1, 0:4], state.at[pairs + 1, 0:4], rim_s.at[0], rim_r.at[0], left
    )
    rim_right0 = remote(state.at[pairs, 0:4], state.at[0, 0:4], rim_s.at[1], rim_r.at[1], right)
    rim_left1 = remote(mid.at[1], mid.at[pairs + 1], rim_s.at[2], rim_r.at[2], left)
    rim_right1 = remote(mid.at[pairs], mid.at[0], rim_s.at[3], rim_r.at[3], right)

    barrier = pltpu.get_barrier_semaphore()
    for device in (peer, left, right, beside):
        pl.semaphore_signal(barrier, inc=1, device_id=device, device_id_type=MESH)
    pl.semaphore_wait(barrier, 4)

    lane = lax.broadcasted_iota(jnp.int32, (half_rows, lanes), 1)
    is_upper = jnp.full((half_rows, lanes), upper, jnp.int32) == 1
    in_slot = lax.rem(lane, half) // 2
    far = half + 2

    def turn(values, shift):
        return pltpu.roll(values, lax.rem(shift + 2 * lanes, lanes), 1)

    def pack(p):
        for copy in loads(p):
            copy.wait()
        for f in range(7):
            if f < 3:
                even, odd = adj[f, 2 * p], adj[f, 2 * p + 1]
            elif f == 3:
                even, odd = visc[2 * p], visc[2 * p + 1]
            else:
                even, odd = flow[f - 4, 2 * p], flow[f - 4, 2 * p + 1]
            lows = jnp.where(lane < half, even, pltpu.roll(odd, half, 1))
            highs = jnp.where(lane < half, pltpu.roll(even, half, 1), odd)
            keep = jnp.where(is_upper, highs, lows)
            give = jnp.where(is_upper, lows, highs)
            state[p + 1, f, mine, :] = keep
            send[p, f] = give
            if f < 4:
                k = f * pairs + p
                slot = in_slot == k
                near_shift = 2 * k + far * upper
                far_shift = 2 * k + far * (1 - upper)
                edges[0, mine, :] = jnp.where(slot, turn(give, near_shift), edges[0, mine, :])
                edges[1, mine, :] = jnp.where(slot, turn(keep, near_shift), edges[1, mine, :])
                edge_out[0] = jnp.where(slot, turn(keep, far_shift), edge_out[0])
                edge_out[1] = jnp.where(slot, turn(give, far_shift), edge_out[1])

    zeros = jnp.zeros((half_rows, lanes), F32)
    for s in range(2):
        edges[s, mine, :] = zeros
        edge_out[s] = zeros
    pack(0)
    swap(0).start()

    @pl.loop(1, pairs)
    def _(i):
        p = pairs - i
        pack(p)

        @pl.when(i <= 1)
        def _():
            swap(p).start()

    swap_edges.start()
    swap(pairs - 2).start()
    swap(1).start()

    for s, source in enumerate((first_m, second_m)):
        values = source[...]
        high = values.astype(BF16)
        low = (values - high.astype(F32)).astype(BF16)
        block = slice(s * rows, (s + 1) * rows)
        matrix[block, 0:rows] = high
        matrix[block, rows : 2 * rows] = high
        matrix[block, 2 * rows : 3 * rows] = low
    edges1[...] = jnp.zeros(edges1.shape, F32)

    def split(source, place, count):
        for c in range(count):
            values = source[place, c]
            high = values.astype(BF16)
            low = (values - high.astype(F32)).astype(BF16)
            columns = slice(c * lanes, (c + 1) * lanes)
            rhs[0:rows, columns] = high
            rhs[rows : 2 * rows, columns] = low
            rhs[2 * rows : 3 * rows, columns] = high
        width = count * lanes
        derived[:, 0:width] = jnp.dot(
            matrix[...], rhs[:, 0:width], preferred_element_type=F32
        )

    clane = lax.broadcasted_iota(jnp.int32, (chunk, lanes), 1)
    crow = lax.broadcasted_iota(jnp.int32, (chunk, lanes), 0)
    lower_lanes = clane < half
    in_half = lax.rem(clane, half)
    cslot = lax.rem(clane, half) // 2

    def join_rims():
        choose = jnp.full((rows, lanes), upper, jnp.int32) == 1
        rim_lo[...] = jnp.where(choose, edges[0], outer[...])
        rim_hi[...] = jnp.where(choose, outer[...], edges[0])

    def join_rims1(g):
        rim1_lo[g] = jnp.where(is_upper, inner1[g], outer1[g])
        rim1_hi[g] = jnp.where(is_upper, outer1[g], inner1[g])

    def rim1_place(p, c, r):
        g = jnp.where(p < early, 0, 1)
        count = jnp.where(p < early, early, pairs - early)
        h = r * chunk // half_rows
        k = c * count + p - g * early + h * (3 * count)
        return g, k, pl.ds(pl.multiple_of(r * chunk - h * half_rows, chunk), chunk)

    def x_views(current, before, after):
        east = pltpu.roll(jnp.where(lower_lanes, after, current), half, 1)
        west = pltpu.roll(jnp.where(lower_lanes, current, before), half, 1)
        return east, west

    def z_rims(low, high, k):
        return turn(low, lanes - 2 - 2 * k), turn(high, half - 2 * k)

    def z_views(current, rims, step):
        under = jnp.where(in_half >= half - step, rims[0], current)
        over = jnp.where(in_half < step, rims[1], current)
        return pltpu.roll(under, step, 1), pltpu.roll(over, lanes - step, 1)

    def coefficients(p):
        @pl.loop(0, rows // chunk)
        def _(r):
            at = pl.ds(pl.multiple_of(r * chunk, chunk), chunk)
            centre = state[p + 1, 3, at, :]
            east, west = x_views(centre, state[p, 3, at, :], state[p + 2, 3, at, :])
            lower, above = z_views(
                centre, z_rims(rim_lo[at, :], rim_hi[at, :], 3 * pairs + p), 1
            )
            ve, vw = 0.05 * (centre + east), 0.05 * (centre + west)
            vu, vl = 0.05 * (centre + above), 0.05 * (centre + lower)
            bx, by, bz = state[p + 1, 4, at, :], state[p + 1, 5, at, :], state[p + 1, 6, at, :]
            bx6, bz6 = bx * (1.0 / 6.0), bz * (1.0 / 6.0)
            coef[p, 0, at, :] = 1.0 - (ve + vw) - (vu + vl)
            coef[p, 1, at, :] = pltpu.roll(bx6 + ve, half, 1)
            coef[p, 2, at, :] = pltpu.roll(vw - bx6, half, 1)
            coef[p, 3, at, :] = bx * (1.0 / 48.0)
            coef[p, 4, at, :] = bz6 + vu
            coef[p, 5, at, :] = vl - bz6
            coef[p, 6, at, :] = bz * (1.0 / 48.0)
            coef[p, 7, at, :] = 0.25 * by + 0.1 * derived[at, 3 * lanes : 4 * lanes]
            coef[p, 8, at, :] = 0.1 * centre

    def advance(source, p, target, place, is_first):
        @pl.loop(0, rows // chunk)
        def _(r):
            at = pl.ds(pl.multiple_of(r * chunk, chunk), chunk)
            at2 = pl.ds(pl.multiple_of(rows + r * chunk, chunk), chunk)
            row = crow + r * chunk
            inside = (row > 0) & (row < rows - 1)
            cs = [coef[p, n, at, :] for n in range(9)]
            for c in range(3):
                g, k1, at1 = rim1_place(p, c, r)
                current = source[p + 1, c, at, :]
                before, after = source[p, c, at, :], source[p + 2, c, at, :]
                beside_x = pltpu.roll(
                    cs[1] * jnp.where(lower_lanes, after, current)
                    + cs[2] * jnp.where(lower_lanes, current, before),
                    half,
                    1,
                )
                if is_first:
                    rims = z_rims(rim_lo[at, :], rim_hi[at, :], c * pairs + p)
                else:
                    rims = z_rims(rim1_lo[g, at1, :], rim1_hi[g, at1, :], k1)
                lower, above = z_views(current, rims, 1)
                lower2, above2 = z_views(current, rims, 2)
                columns = slice(c * lanes, (c + 1) * lanes)
                value = (
                    cs[0] * current
                    + beside_x
                    + cs[3] * (before - after)
                    + cs[4] * above
                    + cs[5] * lower
                    + cs[6] * (lower2 - above2)
                    + cs[7] * derived[at, columns]
                    + cs[8] * derived[at2, columns]
                )
                value = jnp.where(inside, value, 0.0)
                target[place, c, at, :] = value
                if is_first:
                    slot = cslot == k1
                    for e, shift in ((0, far * (1 - upper)), (1, far * upper)):
                        edges1[g, e, at1, :] = jnp.where(
                            slot, turn(value, 2 * k1 + shift), edges1[g, e, at1, :]
                        )

    def second_step(p):
        split(mid, p + 1, 3)
        advance(mid, p, late, p, False)
        give_back(p).start()

    swap(0).wait_recv()
    rim_left0.start()
    swap(pairs - 1).wait_recv()
    rim_right0.start()
    swap_edges.wait_recv()
    pass_edge.start()
    pass_edge.wait_recv()
    join_rims()

    @pl.loop(0, pairs)
    def _(i):
        p = jnp.where(i == 0, pairs - 1, i - 1)

        @pl.when(i == 0)
        def _():
            swap(pairs - 2).wait_recv()
            rim_left0.wait_recv()

        @pl.when(i == 1)
        def _():
            swap(1).wait_recv()
            rim_right0.wait_recv()

        @pl.when((i >= 2) & (i < pairs - 2))
        def _():
            swap(i).wait_recv()

        @pl.when(i < early)
        def _():
            swap(i + 2).start()

        split(state, p + 1, 4)
        coefficients(p)
        advance(state, p, mid, p + 1, True)

        @pl.when(i == 0)
        def _():
            rim_right1.start()

        @pl.when(i == 1)
        def _():
            rim_left1.start()

        @pl.when(i == early)
        def _():
            for copy in edge_copies(0):
                copy.start()
            swap(pairs - 3).start()

        @pl.when(i == early + 1)
        def _():
            for copy in edge_copies(0):
                copy.wait_recv()
            join_rims1(0)
            rim_right1.wait_recv()

            @pl.loop(0, early)
            def _(q):
                second_step(q)

    for copy in edge_copies(1):
        copy.start()
    for copy in edge_copies(1):
        copy.wait_recv()
    join_rims1(1)
    rim_left1.wait_recv()

    @pl.loop(early, pairs)
    def _(p):
        second_step(p)

    @pl.loop(0, pairs)
    def _(p):
        give_back(p).wait_recv()
        for c in range(3):
            keep = late[p, c, mine, :]
            got = back[p, c]
            lows = jnp.where(is_upper, got, keep)
            highs = jnp.where(is_upper, keep, got)
            out[c, 2 * p] = jnp.where(lane < half, lows, pltpu.roll(highs, half, 1))
            out[c, 2 * p + 1] = jnp.where(lane < half, pltpu.roll(lows, half, 1), highs)
        store(p).start()

    @pl.loop(0, pairs)
    def _(p):
        swap(p).wait_send()
        give_back(p).wait_send()
        store(p).wait()

    for copy in (
        swap_edges, pass_edge, *edge_copies(0), *edge_copies(1),
        rim_left0, rim_right0, rim_left1, rim_right1,
    ):
        copy.wait_send()


def per_device(adjoint, base_flow, viscosity, first_matrix, second_matrix):
    _, cells, half_rows, lanes = adjoint.shape
    rows, pairs = 2 * half_rows, cells // 2
    plane = (rows, lanes)
    vmem = pl.BlockSpec(memory_space=pltpu.VMEM)
    anywhere = pl.BlockSpec(memory_space=pl.ANY)
    dma = pltpu.SemaphoreType.DMA
    return pl.pallas_call(
        kernel,
        out_shape=jax.ShapeDtypeStruct(adjoint.shape, F32),
        in_specs=[anywhere] * 3 + [vmem] * 2,
        out_specs=anywhere,
        scratch_shapes=[
            pltpu.VMEM(adjoint.shape, F32),
            pltpu.VMEM(base_flow.shape, F32),
            pltpu.VMEM(viscosity.shape, F32),
            pltpu.VMEM(adjoint.shape, F32),
            pltpu.VMEM((pairs, 7, half_rows, lanes), F32),
            pltpu.VMEM((pairs + 2, 7) + plane, F32),
            pltpu.VMEM((pairs + 2, 3) + plane, F32),
            pltpu.VMEM((pairs, 9) + plane, F32),
            pltpu.VMEM((pairs, 3) + plane, F32),
            pltpu.VMEM((pairs, 3, half_rows, lanes), F32),
            pltpu.VMEM((2 * rows, 3 * rows), BF16),
            pltpu.VMEM((3 * rows, 4 * lanes), BF16),
            pltpu.VMEM((2 * rows, 4 * lanes), F32),
            pltpu.VMEM((2, half_rows, lanes), F32),
            pltpu.VMEM((2,) + plane, F32),
            pltpu.VMEM(plane, F32),
            pltpu.VMEM(plane, F32),
            pltpu.VMEM(plane, F32),
            pltpu.VMEM((2, 2, half_rows, lanes), F32),
            pltpu.VMEM((2, half_rows, lanes), F32),
            pltpu.VMEM((2, half_rows, lanes), F32),
            pltpu.VMEM((2, half_rows, lanes), F32),
            pltpu.VMEM((2, half_rows, lanes), F32),
            dma((pairs,)), dma((pairs,)),
            dma((6,)), dma((6,)),
            dma((4,)), dma((4,)),
            dma((pairs,)), dma((pairs,)),
            dma((3, pairs)), dma((pairs,)),
        ],
        compiler_params=pltpu.CompilerParams(
            collective_id=0, has_side_effects=True, vmem_limit_bytes=56 * 1024 * 1024
        ),
        name="adjoint_steps",
    )(adjoint, base_flow, viscosity, first_matrix, second_matrix)


def solution(mesh):
    return jax.shard_map(
        per_device,
        mesh=mesh,
        in_specs=(
            P(None, "gx", "gy", "gz"),
            P(None, "gx", "gy", "gz"),
            P("gx", "gy", "gz"),
            P(),
            P(),
        ),
        out_specs=P(None, "gx", "gy", "gz"),
        check_vma=False,
    )
```

```python
import jax
import jax.numpy as jnp
from jax import lax
from jax.experimental import pallas as pl
from jax.experimental.pallas import tpu as pltpu
from jax.sharding import PartitionSpec as P

STEPS = 2
MESH = pl.DeviceIdType.MESH
F32 = jnp.float32
BF16 = jnp.bfloat16


def kernel(
    adj_in, flow_in, visc_in, first_m, second_m, out_hbm,
    adj, flow, visc, out,
    send, state, mid, coef, late, back, matrix, rhs, derived,
    edge_out, edges, outer, rim_lo, rim_hi, edges1, inner1, outer1, rim1_lo, rim1_hi,
    swap_s, swap_r, edge_s, edge_r, rim_s, rim_r, ret_s, ret_r, load_s, store_s,
):
    _, cells, half_rows, lanes = adj_in.shape
    rows = 2 * half_rows
    half = lanes // 2
    pairs = cells // 2
    chunk = 32
    early = pairs * 3 // 8
    ngx, ngz = lax.axis_size("gx"), lax.axis_size("gz")
    gy, gx, gz = lax.axis_index("gy"), lax.axis_index("gx"), lax.axis_index("gz")
    upper = lax.rem(gy + gz, 2)
    peer = (1 - gy, gx, gz)
    left = (gy, lax.rem(gx + ngx - 1, ngx), gz)
    right = (gy, lax.rem(gx + 1, ngx), gz)
    beside = (gy, gx, lax.rem(gz + ngz - 1 + 2 * upper, ngz))
    mine = pl.ds(pl.multiple_of(gy * half_rows, half_rows), half_rows)
    other = pl.ds(pl.multiple_of((1 - gy) * half_rows, half_rows), half_rows)

    def remote(src, dst, s, r, device):
        return pltpu.make_async_remote_copy(
            src_ref=src, dst_ref=dst, send_sem=s, recv_sem=r, device_id=device, device_id_type=MESH
        )

    def swap(p):
        return remote(send.at[p], state.at[p + 1, :, mine, :], swap_s.at[p], swap_r.at[p], peer)

    def give_back(p):
        return remote(late.at[p, :, other, :], back.at[p], ret_s.at[p], ret_r.at[p], peer)

    swap_edges = remote(edge_out, edges.at[:, mine, :], edge_s.at[0], edge_r.at[0], peer)
    pass_edge = remote(edges.at[1], outer, edge_s.at[1], edge_r.at[1], beside)

    def edge_copies(g):
        s, r = edge_s.at[2 + 2 * g], edge_r.at[2 + 2 * g]
        inner = remote(edges1.at[g, 0], inner1.at[g], s, r, peer)
        s, r = edge_s.at[3 + 2 * g], edge_r.at[3 + 2 * g]
        return inner, remote(edges1.at[g, 1], outer1.at[g], s, r, beside)

    def loads(p):
        cells_of = pl.ds(2 * p, 2)
        return (
            pltpu.make_async_copy(adj_in.at[:, cells_of], adj.at[:, cells_of], load_s.at[0, p]),
            pltpu.make_async_copy(visc_in.at[cells_of], visc.at[cells_of], load_s.at[1, p]),
            pltpu.make_async_copy(flow_in.at[:, cells_of], flow.at[:, cells_of], load_s.at[2, p]),
        )

    def store(p):
        cells_of = pl.ds(2 * p, 2)
        return pltpu.make_async_copy(out.at[:, cells_of], out_hbm.at[:, cells_of], store_s.at[p])

    for copy in loads(0):
        copy.start()

    @pl.loop(1, pairs)
    def _(i):
        for copy in loads(pairs - i):
            copy.start()

    rim_left0 = remote(
        state.at[1, 0:4], state.at[pairs + 1, 0:4], rim_s.at[0], rim_r.at[0], left
    )
    rim_right0 = remote(state.at[pairs, 0:4], state.at[0, 0:4], rim_s.at[1], rim_r.at[1], right)
    rim_left1 = remote(mid.at[1], mid.at[pairs + 1], rim_s.at[2], rim_r.at[2], left)
    rim_right1 = remote(mid.at[pairs], mid.at[0], rim_s.at[3], rim_r.at[3], right)

    barrier = pltpu.get_barrier_semaphore()
    for device in (peer, left, right, beside):
        pl.semaphore_signal(barrier, inc=1, device_id=device, device_id_type=MESH)
    pl.semaphore_wait(barrier, 4)

    lane = lax.broadcasted_iota(jnp.int32, (half_rows, lanes), 1)
    is_upper = jnp.full((half_rows, lanes), upper, jnp.int32) == 1
    in_slot = lax.rem(lane, half) // 2
    far = half + 2

    def turn(values, shift):
        return pltpu.roll(values, lax.rem(shift + 2 * lanes, lanes), 1)

    def pack(p):
        for copy in loads(p):
            copy.wait()
        for f in range(7):
            if f < 3:
                even, odd = adj[f, 2 * p], adj[f, 2 * p + 1]
            elif f == 3:
                even, odd = visc[2 * p], visc[2 * p + 1]
            else:
                even, odd = flow[f - 4, 2 * p], flow[f - 4, 2 * p + 1]
            lows = jnp.where(lane < half, even, pltpu.roll(odd, half, 1))
            highs = jnp.where(lane < half, pltpu.roll(even, half, 1), odd)
            keep = jnp.where(is_upper, highs, lows)
            give = jnp.where(is_upper, lows, highs)
            state[p + 1, f, mine, :] = keep
            send[p, f] = give
            if f < 4:
                k = f * pairs + p
                slot = in_slot == k
                near_shift = 2 * k + far * upper
                far_shift = 2 * k + far * (1 - upper)
                edges[0, mine, :] = jnp.where(slot, turn(give, near_shift), edges[0, mine, :])
                edges[1, mine, :] = jnp.where(slot, turn(keep, near_shift), edges[1, mine, :])
                edge_out[0] = jnp.where(slot, turn(keep, far_shift), edge_out[0])
                edge_out[1] = jnp.where(slot, turn(give, far_shift), edge_out[1])

    zeros = jnp.zeros((half_rows, lanes), F32)
    for s in range(2):
        edges[s, mine, :] = zeros
        edge_out[s] = zeros
    pack(0)
    swap(0).start()

    @pl.loop(1, pairs)
    def _(i):
        p = pairs - i
        pack(p)

        @pl.when(i <= 1)
        def _():
            swap(p).start()

    swap_edges.start()
    swap(pairs - 2).start()
    swap(1).start()

    for s, source in enumerate((first_m, second_m)):
        values = source[...]
        high = values.astype(BF16)
        low = (values - high.astype(F32)).astype(BF16)
        block = slice(s * rows, (s + 1) * rows)
        matrix[block, 0:rows] = high
        matrix[block, rows : 2 * rows] = high
        matrix[block, 2 * rows : 3 * rows] = low
    edges1[...] = jnp.zeros(edges1.shape, F32)

    def split(source, place, count):
        for c in range(count):
            values = source[place, c]
            high = values.astype(BF16)
            low = (values - high.astype(F32)).astype(BF16)
            columns = slice(c * lanes, (c + 1) * lanes)
            rhs[0:rows, columns] = high
            rhs[rows : 2 * rows, columns] = low
            rhs[2 * rows : 3 * rows, columns] = high
        width = count * lanes
        derived[:, 0:width] = jnp.dot(
            matrix[...], rhs[:, 0:width], preferred_element_type=F32
        )

    clane = lax.broadcasted_iota(jnp.int32, (chunk, lanes), 1)
    crow = lax.broadcasted_iota(jnp.int32, (chunk, lanes), 0)
    lower_lanes = clane < half
    in_half = lax.rem(clane, half)
    cslot = lax.rem(clane, half) // 2

    def join_rims():
        choose = jnp.full((rows, lanes), upper, jnp.int32) == 1
        rim_lo[...] = jnp.where(choose, edges[0], outer[...])
        rim_hi[...] = jnp.where(choose, outer[...], edges[0])

    def join_rims1(g):
        rim1_lo[g] = jnp.where(is_upper, inner1[g], outer1[g])
        rim1_hi[g] = jnp.where(is_upper, outer1[g], inner1[g])

    def rim1_place(p, c, r):
        g = jnp.where(p < early, 0, 1)
        count = jnp.where(p < early, early, pairs - early)
        h = r * chunk // half_rows
        k = c * count + p - g * early + h * (3 * count)
        return g, k, pl.ds(pl.multiple_of(r * chunk - h * half_rows, chunk), chunk)

    def x_views(current, before, after):
        east = pltpu.roll(jnp.where(lower_lanes, after, current), half, 1)
        west = pltpu.roll(jnp.where(lower_lanes, current, before), half, 1)
        return east, west

    def z_rims(low, high, k):
        return turn(low, lanes - 2 - 2 * k), turn(high, half - 2 * k)

    def z_views(current, rims, step):
        under = jnp.where(in_half >= half - step, rims[0], current)
        over = jnp.where(in_half < step, rims[1], current)
        return pltpu.roll(under, step, 1), pltpu.roll(over, lanes - step, 1)

    def coefficients(p):
        @pl.loop(0, rows // chunk)
        def _(r):
            at = pl.ds(pl.multiple_of(r * chunk, chunk), chunk)
            centre = state[p + 1, 3, at, :]
            east, west = x_views(centre, state[p, 3, at, :], state[p + 2, 3, at, :])
            lower, above = z_views(
                centre, z_rims(rim_lo[at, :], rim_hi[at, :], 3 * pairs + p), 1
            )
            ve, vw = 0.05 * (centre + east), 0.05 * (centre + west)
            vu, vl = 0.05 * (centre + above), 0.05 * (centre + lower)
            bx, by, bz = state[p + 1, 4, at, :], state[p + 1, 5, at, :], state[p + 1, 6, at, :]
            bx6, bz6 = bx * (1.0 / 6.0), bz * (1.0 / 6.0)
            coef[p, 0, at, :] = 1.0 - (ve + vw) - (vu + vl)
            coef[p, 1, at, :] = pltpu.roll(bx6 + ve, half, 1)
            coef[p, 2, at, :] = pltpu.roll(vw - bx6, half, 1)
            coef[p, 3, at, :] = bx * (1.0 / 48.0)
            coef[p, 4, at, :] = bz6 + vu
            coef[p, 5, at, :] = vl - bz6
            coef[p, 6, at, :] = bz * (1.0 / 48.0)
            coef[p, 7, at, :] = 0.25 * by + 0.1 * derived[at, 3 * lanes : 4 * lanes]
            coef[p, 8, at, :] = 0.1 * centre

    def advance(source, p, target, place, is_first):
        @pl.loop(0, rows // chunk)
        def _(r):
            at = pl.ds(pl.multiple_of(r * chunk, chunk), chunk)
            at2 = pl.ds(pl.multiple_of(rows + r * chunk, chunk), chunk)
            row = crow + r * chunk
            inside = (row > 0) & (row < rows - 1)
            cs = [coef[p, n, at, :] for n in range(9)]
            for c in range(3):
                g, k1, at1 = rim1_place(p, c, r)
                current = source[p + 1, c, at, :]
                before, after = source[p, c, at, :], source[p + 2, c, at, :]
                beside_x = pltpu.roll(
                    cs[1] * jnp.where(lower_lanes, after, current)
                    + cs[2] * jnp.where(lower_lanes, current, before),
                    half,
                    1,
                )
                if is_first:
                    rims = z_rims(rim_lo[at, :], rim_hi[at, :], c * pairs + p)
                else:
                    rims = z_rims(rim1_lo[g, at1, :], rim1_hi[g, at1, :], k1)
                lower, above = z_views(current, rims, 1)
                lower2, above2 = z_views(current, rims, 2)
                columns = slice(c * lanes, (c + 1) * lanes)
                value = (
                    cs[0] * current
                    + beside_x
                    + cs[3] * (before - after)
                    + cs[4] * above
                    + cs[5] * lower
                    + cs[6] * (lower2 - above2)
                    + cs[7] * derived[at, columns]
                    + cs[8] * derived[at2, columns]
                )
                value = jnp.where(inside, value, 0.0)
                target[place, c, at, :] = value
                if is_first:
                    slot = cslot == k1
                    for e, shift in ((0, far * (1 - upper)), (1, far * upper)):
                        edges1[g, e, at1, :] = jnp.where(
                            slot, turn(value, 2 * k1 + shift), edges1[g, e, at1, :]
                        )

    def second_step(p):
        split(mid, p + 1, 3)
        advance(mid, p, late, p, False)
        give_back(p).start()

    swap(0).wait_recv()
    rim_left0.start()
    swap(pairs - 1).wait_recv()
    rim_right0.start()
    swap_edges.wait_recv()
    pass_edge.start()
    pass_edge.wait_recv()
    join_rims()

    @pl.loop(0, pairs)
    def _(i):
        p = jnp.where(i == 0, pairs - 1, i - 1)

        @pl.when(i == 0)
        def _():
            swap(pairs - 2).wait_recv()
            rim_left0.wait_recv()

        @pl.when(i == 1)
        def _():
            swap(1).wait_recv()
            rim_right0.wait_recv()

        @pl.when((i >= 2) & (i < pairs - 2))
        def _():
            swap(i).wait_recv()

        @pl.when(i < early)
        def _():
            swap(i + 2).start()

        split(state, p + 1, 4)
        coefficients(p)
        advance(state, p, mid, p + 1, True)

        @pl.when(i == 0)
        def _():
            rim_right1.start()

        @pl.when(i == 1)
        def _():
            rim_left1.start()

        @pl.when(i == early)
        def _():
            for copy in edge_copies(0):
                copy.start()
            swap(pairs - 3).start()

        @pl.when(i == early + 1)
        def _():
            for copy in edge_copies(0):
                copy.wait_recv()
            join_rims1(0)
            rim_right1.wait_recv()

            @pl.loop(0, early)
            def _(q):
                second_step(q)

    for copy in edge_copies(1):
        copy.start()
    for copy in edge_copies(1):
        copy.wait_recv()
    join_rims1(1)
    rim_left1.wait_recv()

    @pl.loop(early, pairs)
    def _(p):
        second_step(p)

    @pl.loop(0, pairs)
    def _(p):
        give_back(p).wait_recv()
        for c in range(3):
            keep = late[p, c, mine, :]
            got = back[p, c]
            lows = jnp.where(is_upper, got, keep)
            highs = jnp.where(is_upper, keep, got)
            out[c, 2 * p] = jnp.where(lane < half, lows, pltpu.roll(highs, half, 1))
            out[c, 2 * p + 1] = jnp.where(lane < half, pltpu.roll(lows, half, 1), highs)
        store(p).start()

    @pl.loop(0, pairs)
    def _(p):
        swap(p).wait_send()
        give_back(p).wait_send()
        store(p).wait()

    for copy in (
        swap_edges, pass_edge, *edge_copies(0), *edge_copies(1),
        rim_left0, rim_right0, rim_left1, rim_right1,
    ):
        copy.wait_send()


def hand_over(source, target, sems):
    cells = source.shape[1]

    def copy(x):
        return pltpu.make_async_copy(source.at[:, x], target.at[:, x], sems.at[x])

    for x in range(cells):
        copy(x).start()
    for x in range(cells):
        copy(x).wait()


def per_device(adjoint, base_flow, viscosity, first_matrix, second_matrix):
    _, cells, half_rows, lanes = adjoint.shape
    rows, pairs = 2 * half_rows, cells // 2
    plane = (rows, lanes)
    vmem = pl.BlockSpec(memory_space=pltpu.VMEM)
    anywhere = pl.BlockSpec(memory_space=pl.ANY)
    dma = pltpu.SemaphoreType.DMA
    result = pl.pallas_call(
        kernel,
        out_shape=jax.ShapeDtypeStruct(adjoint.shape, F32),
        in_specs=[anywhere] * 3 + [vmem] * 2,
        out_specs=anywhere,
        scratch_shapes=[
            pltpu.VMEM(adjoint.shape, F32),
            pltpu.VMEM(base_flow.shape, F32),
            pltpu.VMEM(viscosity.shape, F32),
            pltpu.VMEM(adjoint.shape, F32),
            pltpu.VMEM((pairs, 7, half_rows, lanes), F32),
            pltpu.VMEM((pairs + 2, 7) + plane, F32),
            pltpu.VMEM((pairs + 2, 3) + plane, F32),
            pltpu.VMEM((pairs, 9) + plane, F32),
            pltpu.VMEM((pairs, 3) + plane, F32),
            pltpu.VMEM((pairs, 3, half_rows, lanes), F32),
            pltpu.VMEM((2 * rows, 3 * rows), BF16),
            pltpu.VMEM((3 * rows, 4 * lanes), BF16),
            pltpu.VMEM((2 * rows, 4 * lanes), F32),
            pltpu.VMEM((2, half_rows, lanes), F32),
            pltpu.VMEM((2,) + plane, F32),
            pltpu.VMEM(plane, F32),
            pltpu.VMEM(plane, F32),
            pltpu.VMEM(plane, F32),
            pltpu.VMEM((2, 2, half_rows, lanes), F32),
            pltpu.VMEM((2, half_rows, lanes), F32),
            pltpu.VMEM((2, half_rows, lanes), F32),
            pltpu.VMEM((2, half_rows, lanes), F32),
            pltpu.VMEM((2, half_rows, lanes), F32),
            dma((pairs,)), dma((pairs,)),
            dma((6,)), dma((6,)),
            dma((4,)), dma((4,)),
            dma((pairs,)), dma((pairs,)),
            dma((3, pairs)), dma((pairs,)),
        ],
        compiler_params=pltpu.CompilerParams(
            collective_id=0, has_side_effects=True, vmem_limit_bytes=56 * 1024 * 1024
        ),
        name="adjoint_steps",
    )(adjoint, base_flow, viscosity, first_matrix, second_matrix)
    return pl.pallas_call(
        hand_over,
        out_shape=jax.ShapeDtypeStruct(adjoint.shape, F32),
        in_specs=[anywhere],
        out_specs=anywhere,
        scratch_shapes=[dma((cells,))],
        compiler_params=pltpu.CompilerParams(vmem_limit_bytes=62 * 1024 * 1024),
        name="hand_over",
    )(result)


def solution(mesh):
    return jax.shard_map(
        per_device,
        mesh=mesh,
        in_specs=(
            P(None, "gx", "gy", "gz"),
            P(None, "gx", "gy", "gz"),
            P("gx", "gy", "gz"),
            P(),
            P(),
        ),
        out_specs=P(None, "gx", "gy", "gz"),
        check_vma=False,
    )
```

```python
import jax
import jax.numpy as jnp
from jax import lax
from jax.experimental import pallas as pl
from jax.experimental.pallas import tpu as pltpu
from jax.sharding import PartitionSpec as P

STEPS = 2
MESH = pl.DeviceIdType.MESH
F32 = jnp.float32
BF16 = jnp.bfloat16


def kernel(
    adj_in, flow_in, visc_in, first_m, second_m, out_hbm,
    adj, flow, visc, out,
    send, state, mid, coef, late, back, matrix, rhs, derived,
    edge_out, edges, outer, rim_lo, rim_hi, edges1, inner1, outer1, rim1_lo, rim1_hi,
    swap_s, swap_r, edge_s, edge_r, rim_s, rim_r, ret_s, ret_r, load_s, store_s,
):
    _, cells, half_rows, lanes = adj_in.shape
    rows = 2 * half_rows
    half = lanes // 2
    pairs = cells // 2
    chunk = 32
    early = pairs * 3 // 8
    ngx, ngz = lax.axis_size("gx"), lax.axis_size("gz")
    gy, gx, gz = lax.axis_index("gy"), lax.axis_index("gx"), lax.axis_index("gz")
    upper = lax.rem(gy + gz, 2)
    peer = (1 - gy, gx, gz)
    left = (gy, lax.rem(gx + ngx - 1, ngx), gz)
    right = (gy, lax.rem(gx + 1, ngx), gz)
    beside = (gy, gx, lax.rem(gz + ngz - 1 + 2 * upper, ngz))
    mine = pl.ds(pl.multiple_of(gy * half_rows, half_rows), half_rows)
    other = pl.ds(pl.multiple_of((1 - gy) * half_rows, half_rows), half_rows)

    def remote(src, dst, s, r, device):
        return pltpu.make_async_remote_copy(
            src_ref=src, dst_ref=dst, send_sem=s, recv_sem=r, device_id=device, device_id_type=MESH
        )

    def swap(p):
        return remote(send.at[p], state.at[p + 1, :, mine, :], swap_s.at[p], swap_r.at[p], peer)

    def give_back(p):
        return remote(late.at[p, :, other, :], back.at[p], ret_s.at[p], ret_r.at[p], peer)

    swap_edges = remote(edge_out, edges.at[:, mine, :], edge_s.at[0], edge_r.at[0], peer)
    pass_edge = remote(edges.at[1], outer, edge_s.at[1], edge_r.at[1], beside)

    def edge_copies(g):
        s, r = edge_s.at[2 + 2 * g], edge_r.at[2 + 2 * g]
        inner = remote(edges1.at[g, 0], inner1.at[g], s, r, peer)
        s, r = edge_s.at[3 + 2 * g], edge_r.at[3 + 2 * g]
        return inner, remote(edges1.at[g, 1], outer1.at[g], s, r, beside)

    def loads(p):
        cells_of = pl.ds(2 * p, 2)
        return (
            pltpu.make_async_copy(adj_in.at[:, cells_of], adj.at[:, cells_of], load_s.at[0, p]),
            pltpu.make_async_copy(visc_in.at[cells_of], visc.at[cells_of], load_s.at[1, p]),
            pltpu.make_async_copy(flow_in.at[:, cells_of], flow.at[:, cells_of], load_s.at[2, p]),
        )

    def store(p):
        cells_of = pl.ds(2 * p, 2)
        return pltpu.make_async_copy(out.at[:, cells_of], out_hbm.at[:, cells_of], store_s.at[p])

    for copy in loads(0):
        copy.start()

    @pl.loop(1, pairs)
    def _(i):
        for copy in loads(pairs - i):
            copy.start()

    rim_left0 = remote(
        state.at[1, 0:4], state.at[pairs + 1, 0:4], rim_s.at[0], rim_r.at[0], left
    )
    rim_right0 = remote(state.at[pairs, 0:4], state.at[0, 0:4], rim_s.at[1], rim_r.at[1], right)
    rim_left1 = remote(mid.at[1], mid.at[pairs + 1], rim_s.at[2], rim_r.at[2], left)
    rim_right1 = remote(mid.at[pairs], mid.at[0], rim_s.at[3], rim_r.at[3], right)

    barrier = pltpu.get_barrier_semaphore()
    for device in (peer, left, right, beside):
        pl.semaphore_signal(barrier, inc=1, device_id=device, device_id_type=MESH)
    pl.semaphore_wait(barrier, 4)

    lane = lax.broadcasted_iota(jnp.int32, (half_rows, lanes), 1)
    is_upper = jnp.full((half_rows, lanes), upper, jnp.int32) == 1
    in_slot = lax.rem(lane, half) // 2
    far = half + 2

    def turn(values, shift):
        return pltpu.roll(values, lax.rem(shift + 2 * lanes, lanes), 1)

    def pack(p):
        for copy in loads(p):
            copy.wait()
        for f in range(7):
            if f < 3:
                even, odd = adj[f, 2 * p], adj[f, 2 * p + 1]
            elif f == 3:
                even, odd = visc[2 * p], visc[2 * p + 1]
            else:
                even, odd = flow[f - 4, 2 * p], flow[f - 4, 2 * p + 1]
            lows = jnp.where(lane < half, even, pltpu.roll(odd, half, 1))
            highs = jnp.where(lane < half, pltpu.roll(even, half, 1), odd)
            keep = jnp.where(is_upper, highs, lows)
            give = jnp.where(is_upper, lows, highs)
            state[p + 1, f, mine, :] = keep
            send[p, f] = give
            if f < 4:
                k = f * pairs + p
                slot = in_slot == k
                near_shift = 2 * k + far * upper
                far_shift = 2 * k + far * (1 - upper)
                edges[0, mine, :] = jnp.where(slot, turn(give, near_shift), edges[0, mine, :])
                edges[1, mine, :] = jnp.where(slot, turn(keep, near_shift), edges[1, mine, :])
                edge_out[0] = jnp.where(slot, turn(keep, far_shift), edge_out[0])
                edge_out[1] = jnp.where(slot, turn(give, far_shift), edge_out[1])

    zeros = jnp.zeros((half_rows, lanes), F32)
    for s in range(2):
        edges[s, mine, :] = zeros
        edge_out[s] = zeros
    pack(0)
    swap(0).start()

    @pl.loop(1, pairs)
    def _(i):
        p = pairs - i
        pack(p)

        @pl.when(i <= 1)
        def _():
            swap(p).start()

    swap_edges.start()
    swap(pairs - 2).start()
    swap(1).start()

    for s, source in enumerate((first_m, second_m)):
        values = source[...]
        high = values.astype(BF16)
        low = (values - high.astype(F32)).astype(BF16)
        block = slice(s * rows, (s + 1) * rows)
        matrix[block, 0:rows] = high
        matrix[block, rows : 2 * rows] = high
        matrix[block, 2 * rows : 3 * rows] = low
    edges1[...] = jnp.zeros(edges1.shape, F32)

    def split(source, place, count):
        for c in range(count):
            values = source[place, c]
            high = values.astype(BF16)
            low = (values - high.astype(F32)).astype(BF16)
            columns = slice(c * lanes, (c + 1) * lanes)
            rhs[0:rows, columns] = high
            rhs[rows : 2 * rows, columns] = low
            rhs[2 * rows : 3 * rows, columns] = high
        width = count * lanes
        derived[:, 0:width] = jnp.dot(
            matrix[...], rhs[:, 0:width], preferred_element_type=F32
        )

    clane = lax.broadcasted_iota(jnp.int32, (chunk, lanes), 1)
    crow = lax.broadcasted_iota(jnp.int32, (chunk, lanes), 0)
    lower_lanes = clane < half
    in_half = lax.rem(clane, half)
    cslot = lax.rem(clane, half) // 2

    def join_rims():
        choose = jnp.full((rows, lanes), upper, jnp.int32) == 1
        rim_lo[...] = jnp.where(choose, edges[0], outer[...])
        rim_hi[...] = jnp.where(choose, outer[...], edges[0])

    def join_rims1(g):
        rim1_lo[g] = jnp.where(is_upper, inner1[g], outer1[g])
        rim1_hi[g] = jnp.where(is_upper, outer1[g], inner1[g])

    def rim1_place(p, c, r):
        g = jnp.where(p < early, 0, 1)
        count = jnp.where(p < early, early, pairs - early)
        h = r * chunk // half_rows
        k = c * count + p - g * early + h * (3 * count)
        return g, k, pl.ds(pl.multiple_of(r * chunk - h * half_rows, chunk), chunk)

    def x_views(current, before, after):
        east = pltpu.roll(jnp.where(lower_lanes, after, current), half, 1)
        west = pltpu.roll(jnp.where(lower_lanes, current, before), half, 1)
        return east, west

    def z_rims(low, high, k):
        return turn(low, lanes - 2 - 2 * k), turn(high, half - 2 * k)

    def z_views(current, rims, step):
        under = jnp.where(in_half >= half - step, rims[0], current)
        over = jnp.where(in_half < step, rims[1], current)
        return pltpu.roll(under, step, 1), pltpu.roll(over, lanes - step, 1)

    def coefficients(p):
        @pl.loop(0, rows // chunk)
        def _(r):
            at = pl.ds(pl.multiple_of(r * chunk, chunk), chunk)
            centre = state[p + 1, 3, at, :]
            east, west = x_views(centre, state[p, 3, at, :], state[p + 2, 3, at, :])
            lower, above = z_views(
                centre, z_rims(rim_lo[at, :], rim_hi[at, :], 3 * pairs + p), 1
            )
            ve, vw = 0.05 * (centre + east), 0.05 * (centre + west)
            vu, vl = 0.05 * (centre + above), 0.05 * (centre + lower)
            bx, by, bz = state[p + 1, 4, at, :], state[p + 1, 5, at, :], state[p + 1, 6, at, :]
            bx6, bz6 = bx * (1.0 / 6.0), bz * (1.0 / 6.0)
            coef[p, 0, at, :] = 1.0 - (ve + vw) - (vu + vl)
            coef[p, 1, at, :] = pltpu.roll(bx6 + ve, half, 1)
            coef[p, 2, at, :] = pltpu.roll(vw - bx6, half, 1)
            coef[p, 3, at, :] = bx * (1.0 / 48.0)
            coef[p, 4, at, :] = bz6 + vu
            coef[p, 5, at, :] = vl - bz6
            coef[p, 6, at, :] = bz * (1.0 / 48.0)
            coef[p, 7, at, :] = 0.25 * by + 0.1 * derived[at, 3 * lanes : 4 * lanes]
            coef[p, 8, at, :] = 0.1 * centre

    def advance(source, p, target, place, is_first):
        @pl.loop(0, rows // chunk)
        def _(r):
            at = pl.ds(pl.multiple_of(r * chunk, chunk), chunk)
            at2 = pl.ds(pl.multiple_of(rows + r * chunk, chunk), chunk)
            row = crow + r * chunk
            inside = (row > 0) & (row < rows - 1)
            cs = [coef[p, n, at, :] for n in range(9)]
            for c in range(3):
                g, k1, at1 = rim1_place(p, c, r)
                current = source[p + 1, c, at, :]
                before, after = source[p, c, at, :], source[p + 2, c, at, :]
                beside_x = pltpu.roll(
                    cs[1] * jnp.where(lower_lanes, after, current)
                    + cs[2] * jnp.where(lower_lanes, current, before),
                    half,
                    1,
                )
                if is_first:
                    rims = z_rims(rim_lo[at, :], rim_hi[at, :], c * pairs + p)
                else:
                    rims = z_rims(rim1_lo[g, at1, :], rim1_hi[g, at1, :], k1)
                lower, above = z_views(current, rims, 1)
                lower2, above2 = z_views(current, rims, 2)
                columns = slice(c * lanes, (c + 1) * lanes)
                value = (
                    cs[0] * current
                    + beside_x
                    + cs[3] * (before - after)
                    + cs[4] * above
                    + cs[5] * lower
                    + cs[6] * (lower2 - above2)
                    + cs[7] * derived[at, columns]
                    + cs[8] * derived[at2, columns]
                )
                value = jnp.where(inside, value, 0.0)
                target[place, c, at, :] = value
                if is_first:
                    slot = cslot == k1
                    for e, shift in ((0, far * (1 - upper)), (1, far * upper)):
                        edges1[g, e, at1, :] = jnp.where(
                            slot, turn(value, 2 * k1 + shift), edges1[g, e, at1, :]
                        )

    def second_step(p):
        split(mid, p + 1, 3)
        advance(mid, p, late, p, False)
        give_back(p).start()

    swap(0).wait_recv()
    rim_left0.start()
    swap(pairs - 1).wait_recv()
    rim_right0.start()
    swap_edges.wait_recv()
    pass_edge.start()
    pass_edge.wait_recv()
    join_rims()

    @pl.loop(0, pairs)
    def _(i):
        p = jnp.where(i == 0, pairs - 1, i - 1)

        @pl.when(i == 0)
        def _():
            swap(pairs - 2).wait_recv()
            rim_left0.wait_recv()

        @pl.when(i == 1)
        def _():
            swap(1).wait_recv()
            rim_right0.wait_recv()

        @pl.when((i >= 2) & (i < pairs - 2))
        def _():
            swap(i).wait_recv()

        @pl.when(i < early)
        def _():
            swap(i + 2).start()

        split(state, p + 1, 4)
        coefficients(p)
        advance(state, p, mid, p + 1, True)

        @pl.when(i == 0)
        def _():
            rim_right1.start()

        @pl.when(i == 1)
        def _():
            rim_left1.start()

        @pl.when(i == early)
        def _():
            for copy in edge_copies(0):
                copy.start()
            swap(pairs - 3).start()

        @pl.when(i == early + 1)
        def _():
            for copy in edge_copies(0):
                copy.wait_recv()
            join_rims1(0)
            rim_right1.wait_recv()

            @pl.loop(0, early)
            def _(q):
                second_step(q)

    for copy in edge_copies(1):
        copy.start()
    for copy in edge_copies(1):
        copy.wait_recv()
    join_rims1(1)
    rim_left1.wait_recv()

    @pl.loop(early, pairs)
    def _(p):
        second_step(p)

    @pl.loop(0, pairs)
    def _(p):
        give_back(p).wait_recv()
        for c in range(3):
            keep = late[p, c, mine, :]
            got = back[p, c]
            lows = jnp.where(is_upper, got, keep)
            highs = jnp.where(is_upper, keep, got)
            out[c, 2 * p] = jnp.where(lane < half, lows, pltpu.roll(highs, half, 1))
            out[c, 2 * p + 1] = jnp.where(lane < half, pltpu.roll(lows, half, 1), highs)
        store(p).start()

    @pl.loop(0, pairs)
    def _(p):
        swap(p).wait_send()
        give_back(p).wait_send()
        store(p).wait()

    for copy in (
        swap_edges, pass_edge, *edge_copies(0), *edge_copies(1),
        rim_left0, rim_right0, rim_left1, rim_right1,
    ):
        copy.wait_send()


def hand_over(source, target):
    target[...] = source[...]


def per_device(adjoint, base_flow, viscosity, first_matrix, second_matrix):
    _, cells, half_rows, lanes = adjoint.shape
    rows, pairs = 2 * half_rows, cells // 2
    plane = (rows, lanes)
    vmem = pl.BlockSpec(memory_space=pltpu.VMEM)
    anywhere = pl.BlockSpec(memory_space=pl.ANY)
    dma = pltpu.SemaphoreType.DMA
    result = pl.pallas_call(
        kernel,
        out_shape=jax.ShapeDtypeStruct(adjoint.shape, F32),
        in_specs=[anywhere] * 3 + [vmem] * 2,
        out_specs=anywhere,
        scratch_shapes=[
            pltpu.VMEM(adjoint.shape, F32),
            pltpu.VMEM(base_flow.shape, F32),
            pltpu.VMEM(viscosity.shape, F32),
            pltpu.VMEM(adjoint.shape, F32),
            pltpu.VMEM((pairs, 7, half_rows, lanes), F32),
            pltpu.VMEM((pairs + 2, 7) + plane, F32),
            pltpu.VMEM((pairs + 2, 3) + plane, F32),
            pltpu.VMEM((pairs, 9) + plane, F32),
            pltpu.VMEM((pairs, 3) + plane, F32),
            pltpu.VMEM((pairs, 3, half_rows, lanes), F32),
            pltpu.VMEM((2 * rows, 3 * rows), BF16),
            pltpu.VMEM((3 * rows, 4 * lanes), BF16),
            pltpu.VMEM((2 * rows, 4 * lanes), F32),
            pltpu.VMEM((2, half_rows, lanes), F32),
            pltpu.VMEM((2,) + plane, F32),
            pltpu.VMEM(plane, F32),
            pltpu.VMEM(plane, F32),
            pltpu.VMEM(plane, F32),
            pltpu.VMEM((2, 2, half_rows, lanes), F32),
            pltpu.VMEM((2, half_rows, lanes), F32),
            pltpu.VMEM((2, half_rows, lanes), F32),
            pltpu.VMEM((2, half_rows, lanes), F32),
            pltpu.VMEM((2, half_rows, lanes), F32),
            dma((pairs,)), dma((pairs,)),
            dma((6,)), dma((6,)),
            dma((4,)), dma((4,)),
            dma((pairs,)), dma((pairs,)),
            dma((3, pairs)), dma((pairs,)),
        ],
        compiler_params=pltpu.CompilerParams(
            collective_id=0, has_side_effects=True, vmem_limit_bytes=56 * 1024 * 1024
        ),
        name="adjoint_steps",
    )(adjoint, base_flow, viscosity, first_matrix, second_matrix)
    block = pl.BlockSpec((3, 4, half_rows, lanes), lambda x: (0, x, 0, 0))
    return pl.pallas_call(
        hand_over,
        out_shape=jax.ShapeDtypeStruct(adjoint.shape, F32),
        grid=(cells // 4,),
        in_specs=[block],
        out_specs=block,
        compiler_params=pltpu.CompilerParams(vmem_limit_bytes=62 * 1024 * 1024),
        name="hand_over",
    )(result)


def solution(mesh):
    return jax.shard_map(
        per_device,
        mesh=mesh,
        in_specs=(
            P(None, "gx", "gy", "gz"),
            P(None, "gx", "gy", "gz"),
            P("gx", "gy", "gz"),
            P(),
            P(),
        ),
        out_specs=P(None, "gx", "gy", "gz"),
        check_vma=False,
    )
```
